512 devices in a mesh: seq: 32 (over x, z_lo, core), head: 16 (over y, z_hi).
Axes of the slice: x: 4, y: 4, z: 16 (z_hi: 4, z_lo: 4; z = z_hi * 4 + z_lo), core: 2. Of those that a mesh axis runs over, the one named last changes fastest.
Arguments:
- queries: bfloat16 [65536, 4096], P('seq', 'head'), may hold values from -24 to 24
- key_value_rows: bfloat16 [65536, 2048], P('seq', 'head'), may hold values from -4 to 4
- upstream: bfloat16 [65536, 4096], P('seq', 'head'), may hold values from -6 to 6
- ancestors: int32 [512, 2], P(('seq', 'head')), may hold values from -1 to 510, as said below
- valid: int32 [512, 2], P(('seq', 'head')), may hold values from 0 to 1
- span_lo: int32 [65536], P(('seq', 'head')), may hold values from 0 to 7, as said below
- span_hi: int32 [65536], P(('seq', 'head')), may hold values from 1 to 7, as said below
Outputs:
- grad_queries: bfloat16 [65536, 4096], P('seq', 'head')
- key_value_gradient: bfloat16 [65536, 2048], P('seq', 'head')
The draws below stay inside these ranges and needn't reach their ends.
Inputs may be any that keep to these rules, and one draw needn't show every extreme that they name: For block b and slot a with valid[b, a] = 1, b - 6 <= ancestors[b, a] <= b - 1, and the valid entries of one block are distinct; entries with valid 0 hold -1. `span_lo`: inside each block the tokens form 8 nodes, each a run of consecutive tokens numbered in depth-first order from 0, the first node at least two tokens long and the root of the block's tree. span_lo[t] <= span_hi[t]; tokens of one node share both numbers.
All inputs are finite; a program needn't handle non-finite values.
Results may differ from the reference program's by a relative error of at most 0.02.
Values may be sent and summed in bfloat16 or wider, within the bound.
A program may use at most 64 MiB of HBM per device.

```python
import math
import jax
import jax.numpy as jnp
from jax import lax

QUERY_HEADS = 32
KEY_VALUE_HEADS = 8
HEAD_SIZE = 128
BLOCK_TOKENS = 128
SPAN = 6
NANC = 2
NODES = 8
TOKENS = 65536


def float_fields(key):
    width_total = 2 * KEY_VALUE_HEADS * HEAD_SIZE
    first, second, third = jax.random.split(key, 3)
    row_scale = jnp.exp(jax.random.uniform(third, (TOKENS, 1), jnp.float32, math.log(0.4), math.log(4.0)))
    query_key_pairs = jnp.clip(jax.random.normal(first, (TOKENS, width_total), jnp.float32), -4.0, 4.0)
    asks = jnp.clip(jax.random.normal(second, (TOKENS, QUERY_HEADS * HEAD_SIZE), jnp.float32), -4.0, 4.0) * row_scale
    return (query_key_pairs, asks)


def draw_queries(key, part):
    return float_fields(jax.random.fold_in(key, 9))[1].astype(jnp.bfloat16)


def draw_key_value_rows(key, part):
    return float_fields(jax.random.fold_in(key, 9))[0].astype(jnp.bfloat16)


def ancestry(key):
    block_indices = TOKENS // BLOCK_TOKENS
    subkeys = jax.random.split(key, block_indices + 1)
    offsets = jax.vmap(lambda single: jax.random.permutation(single, SPAN)[:NANC] + 1)(subkeys[1:])
    counts = jax.random.randint(subkeys[0], (block_indices,), 0, NANC + 1)
    block_ids = jnp.arange(block_indices)[:, None]
    listed = block_ids - offsets
    usable = (jnp.arange(NANC)[None, :] < counts[:, None]) & (listed >= 0)
    return (jnp.where(usable, listed, -1).astype(jnp.int32), usable.astype(jnp.int32))


def draw_ancestors(key, part):
    return ancestry(jax.random.fold_in(key, 3))[0]


def draw_valid(key, part):
    return ancestry(jax.random.fold_in(key, 3))[1]


def tree_fields(key):
    block_indices = TOKENS // BLOCK_TOKENS

    def single_block(subkey):
        first, second = jax.random.split(subkey)
        cuts = jax.random.permutation(first, BLOCK_TOKENS - 2)[:NODES - 1] + 2
        places = jnp.arange(BLOCK_TOKENS)
        member = jnp.sum(places[:, None] >= cuts[None, :], axis=1)
        draws = jax.random.randint(second, (NODES - 1,), 0, 1 << 20)

        def grow(depth, value):
            deeper = 1 + value % (depth + 1)
            return (deeper, deeper)
        _, depths = lax.scan(grow, jnp.int32(0), draws)
        depths = jnp.concatenate([jnp.zeros((1,), jnp.int32), depths.astype(jnp.int32)])
        number = jnp.arange(NODES)
        later = (number[None, :] > number[:, None]) & (depths[None, :] <= depths[:, None])
        finish = jnp.min(jnp.where(later, number[None, :], NODES), axis=1) - 1
        return (member.astype(jnp.int32), finish[member].astype(jnp.int32))
    lows, highs = jax.vmap(single_block)(jax.random.split(key, block_indices))
    return (lows.reshape(TOKENS), highs.reshape(TOKENS))


def draw_span_lo(key, part):
    return tree_fields(jax.random.fold_in(key, 5))[0]


def draw_span_hi(key, part):
    return tree_fields(jax.random.fold_in(key, 5))[1]


def block_scale(rng, shape, cuts, least, top_value):
    factor_of, own = 1.0, jax.random.fold_in(rng, 6)
    for axis_at, blocks in cuts:
        heights = jnp.exp(jax.random.uniform(jax.random.fold_in(own, axis_at), (blocks,), jnp.float32, least / len(cuts), top_value / len(cuts)))
        factor_of = factor_of * jnp.repeat(heights, shape[axis_at] // blocks).reshape([-1 if axis == axis_at else 1 for axis in range(len(shape))])
    return factor_of


def centred(own_key, dims, deviation, reach, shards=(), held_as=jnp.bfloat16):
    factor_of = block_scale(own_key, dims, shards, -0.22, 0.18) if shards else 1.0
    result = jax.random.normal(own_key, dims, jnp.float32) * deviation * factor_of
    return jnp.minimum(jnp.maximum(result, -reach), reach).astype(held_as)


def setup_inputs(seed: int = 0) -> dict:
    arg_keys = jax.random.split(jax.random.key(seed), 8)
    queries = draw_queries(jax.random.fold_in(arg_keys[7], 71), 0)
    key_value_rows = draw_key_value_rows(jax.random.fold_in(arg_keys[7], 71), 0)
    upstream = centred(arg_keys[2], (TOKENS, QUERY_HEADS * HEAD_SIZE), 1.0, 6.0, ((0, 32), (1, 16)))
    ancestors = draw_ancestors(jax.random.fold_in(arg_keys[7], 71), 0)
    valid = draw_valid(jax.random.fold_in(arg_keys[7], 71), 0)
    span_lo = draw_span_lo(jax.random.fold_in(arg_keys[7], 71), 0)
    span_hi = draw_span_hi(jax.random.fold_in(arg_keys[7], 71), 0)
    return {"queries": queries, "key_value_rows": key_value_rows, "upstream": upstream, "ancestors": ancestors, "valid": valid, "span_lo": span_lo, "span_hi": span_hi}


def reference(queries, key_value_rows, upstream, ancestors, valid, span_lo, span_hi):
    block_indices = queries.shape[0] // BLOCK_TOKENS
    head_group = QUERY_HEADS // KEY_VALUE_HEADS
    factor = HEAD_SIZE ** -0.5
    query_block_rows = queries.reshape(block_indices, BLOCK_TOKENS, KEY_VALUE_HEADS, head_group, HEAD_SIZE)
    upstream_block_rows = upstream.reshape(block_indices, BLOCK_TOKENS, KEY_VALUE_HEADS, head_group, HEAD_SIZE)
    tile_block_list = key_value_rows.reshape(block_indices, BLOCK_TOKENS, 2, KEY_VALUE_HEADS, HEAD_SIZE)
    low_blocks = span_lo.reshape(block_indices, BLOCK_TOKENS)
    high_blocks = span_hi.reshape(block_indices, BLOCK_TOKENS)
    order = jnp.arange(BLOCK_TOKENS)

    def visit(carry, index):
        query = query_block_rows[index].astype(jnp.float32)
        grads_up = upstream_block_rows[index].astype(jnp.float32)
        listed = valid[index] > 0
        targets = jnp.concatenate([index[None].astype(jnp.int32), jnp.where(listed, ancestors[index], 0).astype(jnp.int32)])
        tile_stack = tile_block_list[targets].astype(jnp.float32)
        keys = tile_stack[:, :, 0]
        values = tile_stack[:, :, 1]
        low = low_blocks[index]
        high = high_blocks[index]
        diagonal = (order[None, :] <= order[:, None]) & (low[None, :] <= low[:, None]) & (low[:, None] <= high[None, :])
        others = jnp.broadcast_to(listed[None, :, None], (BLOCK_TOKENS, NANC, BLOCK_TOKENS))
        mask = jnp.concatenate([diagonal[:, None, :], others], axis=1)
        scores = jnp.einsum("qgrd,tkgd->grqtk", query, keys) * factor
        scores = jnp.where(mask[None, None], scores, -jnp.inf)
        top = jnp.max(scores, axis=(3, 4), keepdims=True)
        exps = jnp.exp(scores - top)
        probs = exps / jnp.sum(exps, axis=(3, 4), keepdims=True)
        weights = lax.optimization_barrier(probs.astype(jnp.bfloat16)).astype(jnp.float32)
        output = jnp.einsum("grqtk,tkgd->qgrd", weights, values).astype(jnp.bfloat16)
        output = lax.optimization_barrier(output).astype(jnp.float32)
        delta = jnp.sum(grads_up * output, axis=3)
        sens = jnp.einsum("qgrd,tkgd->grqtk", grads_up, values)
        slopes = (probs * (sens - jnp.transpose(delta, (1, 2, 0))[:, :, :, None, None])).astype(jnp.bfloat16)
        slopes = lax.optimization_barrier(slopes).astype(jnp.float32)
        grad_query = (jnp.einsum("grqtk,tkgd->qgrd", slopes, keys) * factor).astype(jnp.bfloat16).reshape(BLOCK_TOKENS, QUERY_HEADS * HEAD_SIZE)
        grad_key = jnp.einsum("grqtk,qgrd->tkgd", slopes, query) * factor
        grad_value = jnp.einsum("grqtk,qgrd->tkgd", weights, grads_up)
        grad_tile = jnp.stack([grad_key, grad_value], axis=2)
        carry = carry.at[targets].add(grad_tile)
        return carry, grad_query

    start_offset = jnp.zeros((block_indices, BLOCK_TOKENS, 2, KEY_VALUE_HEADS, HEAD_SIZE), jnp.float32)
    summed_terms, grad_rows = lax.scan(visit, start_offset, jnp.arange(block_indices, dtype=jnp.int32))
    grad_queries = grad_rows.reshape(block_indices * BLOCK_TOKENS, QUERY_HEADS * HEAD_SIZE)
    key_value_gradient = summed_terms.reshape(block_indices * BLOCK_TOKENS, 2 * KEY_VALUE_HEADS * HEAD_SIZE).astype(jnp.bfloat16)
    return grad_queries, key_value_gradient
```

```python
import functools
import math

import jax
import jax.numpy as jnp
from jax import lax
from jax.experimental import pallas as pl
from jax.experimental.pallas import tpu as pltpu
from jax.sharding import PartitionSpec as P

HEAD = 128
BLOCK = 128
SPAN = 6
MESH = pl.DeviceIdType.MESH
CHUNK = 256
VMEM_LIMIT = 48 * 1024 * 1024


def place():
    s, h = lax.axis_index("seq"), lax.axis_index("head")
    return s, h, h // 4, h % 4


def wait_for(ref, sem):
    pltpu.make_async_copy(ref, ref, sem).wait()


def gather_kernel(ns, nh, rows, kv_ref, lo_ref, hi_ref, anc_ref, val_ref, out_ref, meta_ref, buf,
                  load_sem, meta_send, meta_recv, right_send, left_send, chain_recv, y_send, kv_recv, halo_send,
                  halo_recv):
    s, h, y, zh = place()
    chunks = rows // CHUNK
    halo = SPAN * BLOCK
    first_halo = (rows - halo) // CHUNK
    halos = halo // CHUNK
    order = list(range(chunks))[::-1]
    after, before = (s + 1) % ns, (s + ns - 1) % ns

    mine = 2 * (((zh + 1) % 4) // 2) + zh // 3
    load = pltpu.make_async_copy(kv_ref, buf.at[mine], load_sem)
    load.start()

    barrier = pltpu.get_barrier_semaphore()
    for step in range(1, nh):
        pl.semaphore_signal(barrier, inc=1, device_id=(s, (h + step) % nh), device_id_type=MESH)
    pl.semaphore_signal(barrier, inc=1, device_id=(after, h), device_id_type=MESH)
    pl.semaphore_signal(barrier, inc=1, device_id=(before, h), device_id_type=MESH)

    lane = lax.broadcasted_iota(jnp.int32, (8, BLOCK), 1)
    row = lax.broadcasted_iota(jnp.int32, (8, BLOCK), 0)
    scalars = jnp.where(lane == 0, anc_ref[0, 0], 0) + jnp.where(lane == 1, anc_ref[0, 1], 0)
    scalars = scalars + jnp.where(lane == 2, val_ref[0, 0], 0) + jnp.where(lane == 3, val_ref[0, 1], 0)
    fields = jnp.where(row == 0, lo_ref[...], jnp.where(row == 1, hi_ref[...], scalars))
    meta_ref[h] = fields
    load.wait()
    pl.semaphore_wait(barrier, nh + 1)

    def part(c):
        return pl.ds(c * CHUNK, CHUNK)

    def right(c):
        return pltpu.make_async_remote_copy(
            src_ref=buf.at[2 * (zh % 2), part(c)], dst_ref=buf.at[0, part(c)],
            send_sem=right_send.at[c], recv_sem=chain_recv.at[0, c], device_id=(s, (h + 1) % nh), device_id_type=MESH)

    def left(c):
        return pltpu.make_async_remote_copy(
            src_ref=buf.at[2 - zh % 2, part(c)], dst_ref=buf.at[1, part(c)],
            send_sem=left_send.at[c], recv_sem=chain_recv.at[1, c], device_id=(s, (h + nh - 1) % nh),
            device_id_type=MESH)

    kind = y // 2

    def target(slot, c):
        return out_ref.at[kind, pl.ds(halo + c * CHUNK, CHUNK)]

    def along_y(slot, c):
        return pltpu.make_async_remote_copy(
            src_ref=buf.at[slot, part(c)], dst_ref=target(slot, c), send_sem=y_send.at[slot, c],
            recv_sem=kv_recv.at[kind, c], device_id=(s, (2 * (y % 2) + slot) * 4 + zh), device_id_type=MESH)

    def stay(slot, c):
        return pltpu.make_async_copy(buf.at[slot, part(c)], target(slot, c), kv_recv.at[kind, c])

    def to_next(which, c):
        return pltpu.make_async_remote_copy(
            src_ref=out_ref.at[which, pl.ds(halo + c * CHUNK, CHUNK)],
            dst_ref=out_ref.at[which, pl.ds((c - first_halo) * CHUNK, CHUNK)],
            send_sem=halo_send.at[which, c - first_halo], recv_sem=halo_recv.at[which, c - first_halo],
            device_id=(after, h), device_id_type=MESH)

    @pl.when(zh <= 1)
    def _():
        for c in order:
            right(c).start()

    @pl.when(zh >= 2)
    def _():
        for c in order:
            left(c).start()

    def meta_copy(step):
        return pltpu.make_async_remote_copy(
            src_ref=meta_ref.at[h], dst_ref=meta_ref.at[h], send_sem=meta_send.at[step - 1],
            recv_sem=meta_recv.at[step - 1], device_id=(s, (h + step) % nh), device_id_type=MESH)

    for step in range(1, nh):
        meta_copy(step).start()

    home = (0, 3)

    def finish(c):
        for which in range(2):
            wait_for(out_ref.at[which, pl.ds(halo + c * CHUNK, CHUNK)], kv_recv.at[which, c])
            if c >= first_halo:
                to_next(which, c).start()

    for place_in_order, c in enumerate(order):
        for slot in range(2):
            edge = 3 * slot
            relay = 2 - slot

            @pl.when(zh != edge)
            def _():
                wait_for(buf.at[slot, part(c)], chain_recv.at[slot, c])

            @pl.when(zh == relay)
            def _():
                (right if slot == 0 else left)(c).start()

            @pl.when(y == home[slot])
            def _():
                stay(slot, c).start()

            @pl.when(y != home[slot])
            def _():
                along_y(slot, c).start()

        if place_in_order >= 1:
            finish(order[place_in_order - 1])
    finish(order[-1])

    for which in range(2):
        for piece in range(halos):
            wait_for(out_ref.at[which, pl.ds(piece * CHUNK, CHUNK)], halo_recv.at[which, piece])
    for step in range(1, nh):
        source = (h + nh - step) % nh
        wait_for(meta_ref.at[source], meta_recv.at[step - 1])
    for step in range(1, nh):
        meta_copy(step).wait_send()
    for c in order:
        @pl.when(zh != 3)
        def _():
            right(c).wait_send()

        @pl.when(zh != 0)
        def _():
            left(c).wait_send()

        for slot in range(2):
            @pl.when(y != home[slot])
            def _():
                along_y(slot, c).wait_send()
    for which in range(2):
        for c in range(first_halo, chunks):
            to_next(which, c).wait_send()


def attend_kernel(count, meta_s, meta_v, q_ref, up_ref, kv_ref, dq_ref, dkv_ref, halo_ref, acc):
    s = lax.axis_index("seq")
    factor = HEAD ** -0.5
    scale = factor * math.log2(math.e)
    halo = SPAN * BLOCK
    acc[...] = jnp.zeros_like(acc)
    key_at = lax.broadcasted_iota(jnp.int32, (BLOCK, BLOCK), 0)
    query_at = lax.broadcasted_iota(jnp.int32, (BLOCK, BLOCK), 1)

    def visit(i, carry):
        rows = pl.ds(pl.multiple_of(i * BLOCK, BLOCK), BLOCK)
        tiles = [pl.ds(pl.multiple_of((i + SPAN) * BLOCK, BLOCK), BLOCK)]
        used = []
        for slot in range(2):
            ok = meta_s[i, 2, 2 + slot] > 0
            at = jnp.where(ok, meta_s[i, 2, slot] - s * count, i) + SPAN
            at = jnp.clip(at, 0, count + SPAN - 1)
            tiles.append(pl.ds(pl.multiple_of(at * BLOCK, BLOCK), BLOCK))
            used.append(ok)
        q = jnp.concatenate([q_ref[rows, :HEAD], q_ref[rows, HEAD:]], axis=0)
        up = jnp.concatenate([up_ref[rows, :HEAD], up_ref[rows, HEAD:]], axis=0)
        k = jnp.concatenate([kv_ref[0, t, :] for t in tiles], axis=0)
        v = jnp.concatenate([kv_ref[1, t, :] for t in tiles], axis=0)
        nt = (((1,), (1,)), ((), ()))
        tn = (((0,), (0,)), ((), ()))
        scores = lax.dot_general(k, q, nt, preferred_element_type=jnp.float32)
        sens = lax.dot_general(v, up, nt, preferred_element_type=jnp.float32)
        lo_row = meta_v[i, 0:1, :]
        hi_row = meta_v[i, 1:2, :].astype(jnp.float32)
        hi_col = jnp.broadcast_to(hi_row, (BLOCK, BLOCK)).T
        seen = (key_at <= query_at) & (lo_row.astype(jnp.float32) <= hi_col)
        seen = jnp.concatenate([seen, seen], axis=1)
        low = -jnp.inf
        scores = jnp.concatenate(
            [jnp.where(seen, scores[:BLOCK], low)]
            + [scores[BLOCK * (1 + n):BLOCK * (2 + n)] + jnp.where(used[n], 0.0, low) for n in range(2)], axis=0)
        top = jnp.max(scores, axis=0, keepdims=True)
        exps = jnp.exp2((scores - top) * scale)
        inverse = 1.0 / jnp.sum(exps, axis=0, keepdims=True)
        probs = exps * inverse
        delta = jnp.sum(probs * sens, axis=0, keepdims=True)
        weights = probs.astype(jnp.bfloat16)
        slopes = (probs * (sens - delta)).astype(jnp.bfloat16)
        dq = lax.dot_general(slopes, k, tn, preferred_element_type=jnp.float32) * factor
        dq_ref[rows, :HEAD] = dq[:BLOCK].astype(jnp.bfloat16)
        dq_ref[rows, HEAD:] = dq[BLOCK:].astype(jnp.bfloat16)
        dk = jnp.dot(slopes, q, preferred_element_type=jnp.float32)
        dv = jnp.dot(weights, up, preferred_element_type=jnp.float32)
        for n, t in enumerate(tiles):
            acc[0, t, :] += dk[n * BLOCK:(n + 1) * BLOCK]
            acc[1, t, :] += dv[n * BLOCK:(n + 1) * BLOCK]
        return carry

    lax.fori_loop(0, count, visit, 0)
    halo_ref[0] = (acc[0, :halo] * factor).astype(jnp.bfloat16)
    halo_ref[1] = acc[1, :halo].astype(jnp.bfloat16)
    dkv_ref[0] = (acc[0, halo:] * factor).astype(jnp.bfloat16)
    dkv_ref[1] = acc[1, halo:].astype(jnp.bfloat16)


def return_kernel(ns, nh, rows, dkv_ref, halo_ref, out_ref, part_buf, chain_buf, halo_in, halo_sum,
                  halo_send, halo_recv, y_send, y_recv, left_send, right_send, chain_recv):
    s, h, y, zh = place()
    chunks = rows // CHUNK
    halo = SPAN * BLOCK
    first_halo = (rows - halo) // CHUNK
    halos = halo // CHUNK
    after, before = (s + 1) % ns, (s + ns - 1) % ns

    barrier = pltpu.get_barrier_semaphore()
    for step in range(1, 4):
        pl.semaphore_signal(barrier, inc=1, device_id=(s, ((y + step) % 4) * 4 + zh), device_id_type=MESH)
    for step in (1, 3):
        pl.semaphore_signal(barrier, inc=1, device_id=(s, y * 4 + (zh + step) % 4), device_id_type=MESH)
    pl.semaphore_signal(barrier, inc=1, device_id=(after, h), device_id_type=MESH)
    pl.semaphore_signal(barrier, inc=1, device_id=(before, h), device_id_type=MESH)
    pl.semaphore_wait(barrier, 7)

    def part(c):
        return pl.ds(c * CHUNK, CHUNK)

    def to_before(which, piece):
        return pltpu.make_async_remote_copy(
            src_ref=halo_ref.at[which, part(piece)], dst_ref=halo_in.at[which, part(piece)],
            send_sem=halo_send.at[which, piece], recv_sem=halo_recv.at[which, piece],
            device_id=(before, h), device_id_type=MESH)

    for piece in range(halos):
        for which in range(2):
            to_before(which, piece).start()

    slot_of = y % 2

    def source(which, c):
        if c < first_halo:
            return dkv_ref.at[which, part(c)]
        return halo_sum.at[which, part(c - first_halo)]

    def along_y(which, c):
        return pltpu.make_async_remote_copy(
            src_ref=source(which, c), dst_ref=part_buf.at[slot_of, part(c)], send_sem=y_send.at[which, c],
            recv_sem=y_recv.at[slot_of, c], device_id=(s, (2 * which + y // 2) * 4 + zh), device_id_type=MESH)

    def stay(which, c):
        return pltpu.make_async_copy(source(which, c), part_buf.at[slot_of, part(c)], y_recv.at[slot_of, c])

    def left(c):
        return pltpu.make_async_remote_copy(
            src_ref=part_buf.at[0, part(c)], dst_ref=chain_buf.at[0, part(c)],
            send_sem=left_send.at[c], recv_sem=chain_recv.at[0, c], device_id=(s, (h + nh - 1) % nh),
            device_id_type=MESH)

    def right(c):
        return pltpu.make_async_remote_copy(
            src_ref=part_buf.at[1, part(c)], dst_ref=chain_buf.at[1, part(c)],
            send_sem=right_send.at[c], recv_sem=chain_recv.at[1, c], device_id=(s, (h + 1) % nh),
            device_id_type=MESH)

    home = (0, 3)

    def give(c):
        for which in range(2):
            if c >= first_halo:
                piece = c - first_halo
                wait_for(halo_in.at[which, part(piece)], halo_recv.at[which, piece])
                halo_sum[which, part(piece)] = (
                    dkv_ref[which, part(c)].astype(jnp.float32)
                    + halo_in[which, part(piece)].astype(jnp.float32)).astype(jnp.bfloat16)

            @pl.when(y == home[which])
            def _():
                stay(which, c).start()

            @pl.when(y != home[which])
            def _():
                along_y(which, c).start()

    def total(slot, c):
        return (part_buf[slot, part(c)].astype(jnp.float32)
                + chain_buf[slot, part(c)].astype(jnp.float32)).astype(jnp.bfloat16)

    for c in range(first_halo):
        give(c)

    def chain(c):
        for slot in range(2):
            wait_for(part_buf.at[slot, part(c)], y_recv.at[slot, c])

        @pl.when(zh % 2 == 1)
        def _():
            left(c).start()

        @pl.when(zh % 2 == 0)
        def _():
            right(c).start()

        @pl.when(zh == 2)
        def _():
            wait_for(chain_buf.at[0, part(c)], chain_recv.at[0, c])
            part_buf[0, part(c)] = total(0, c)
            left(c).start()

        @pl.when(zh == 1)
        def _():
            wait_for(chain_buf.at[1, part(c)], chain_recv.at[1, c])
            part_buf[1, part(c)] = total(1, c)
            right(c).start()

    def settle(c):
        @pl.when(zh <= 1)
        def _():
            wait_for(chain_buf.at[0, part(c)], chain_recv.at[0, c])

        @pl.when(zh >= 2)
        def _():
            wait_for(chain_buf.at[1, part(c)], chain_recv.at[1, c])

        @pl.when(zh == 0)
        def _():
            out_ref[part(c)] = total(0, c)

        @pl.when(zh == 1)
        def _():
            out_ref[part(c)] = chain_buf[0, part(c)]

        @pl.when(zh == 2)
        def _():
            out_ref[part(c)] = chain_buf[1, part(c)]

        @pl.when(zh == 3)
        def _():
            out_ref[part(c)] = total(1, c)

    for c in range(chunks):
        if c >= 1 and first_halo + c - 1 < chunks:
            give(first_halo + c - 1)
        chain(c)
    for c in range(chunks):
        settle(c)

    for piece in range(halos):
        for which in range(2):
            to_before(which, piece).wait_send()
    for c in range(chunks):
        for which in range(2):
            @pl.when(y != home[which])
            def _():
                along_y(which, c).wait_send()

        @pl.when(zh != 0)
        def _():
            left(c).wait_send()

        @pl.when(zh != 3)
        def _():
            right(c).wait_send()


def solution(mesh):
    ns, nh = mesh.shape["seq"], mesh.shape["head"]

    def on_device(queries, key_value_rows, upstream, ancestors, valid, span_lo, span_hi):
        rows = queries.shape[0]
        count = rows // BLOCK
        halo = SPAN * BLOCK
        chunks, halos = rows // CHUNK, halo // CHUNK
        vmem = pl.BlockSpec(memory_space=pltpu.VMEM)
        smem = pl.BlockSpec(memory_space=pltpu.SMEM)
        dma = pltpu.SemaphoreType.DMA
        kv, meta = pl.pallas_call(
            functools.partial(gather_kernel, ns, nh, rows),
            out_shape=(jax.ShapeDtypeStruct((2, halo + rows, HEAD), jnp.bfloat16),
                       jax.ShapeDtypeStruct((nh, 8, BLOCK), jnp.int32)),
            in_specs=[pl.BlockSpec(memory_space=pl.ANY), vmem, vmem, smem, smem],
            out_specs=(vmem, vmem),
            scratch_shapes=[
                pltpu.VMEM((3, rows, HEAD), jnp.bfloat16),
                dma, dma((nh - 1,)), dma((nh - 1,)), dma((chunks,)), dma((chunks,)), dma((2, chunks)),
                dma((2, chunks)), dma((2, chunks)), dma((2, halos)), dma((2, halos)),
            ],
            compiler_params=pltpu.CompilerParams(
                collective_id=0, has_side_effects=True, vmem_limit_bytes=VMEM_LIMIT),
            name="gather_units",
        )(key_value_rows, span_lo.reshape(1, BLOCK), span_hi.reshape(1, BLOCK), ancestors, valid)
        dq, dkv, dhalo = pl.pallas_call(
            functools.partial(attend_kernel, count),
            out_shape=(jax.ShapeDtypeStruct(queries.shape, jnp.bfloat16),
                       jax.ShapeDtypeStruct((2, rows, HEAD), jnp.bfloat16),
                       jax.ShapeDtypeStruct((2, halo, HEAD), jnp.bfloat16)),
            in_specs=[smem, vmem, vmem, vmem, vmem],
            out_specs=(vmem, vmem, vmem),
            scratch_shapes=[pltpu.VMEM((2, halo + rows, HEAD), jnp.float32)],
            compiler_params=pltpu.CompilerParams(vmem_limit_bytes=VMEM_LIMIT),
            name="attend",
        )(meta, meta, queries, upstream, kv)
        grad_pairs = pl.pallas_call(
            functools.partial(return_kernel, ns, nh, rows),
            out_shape=jax.ShapeDtypeStruct((rows, HEAD), jnp.bfloat16),
            in_specs=[vmem, vmem],
            out_specs=vmem,
            scratch_shapes=[
                pltpu.VMEM((2, rows, HEAD), jnp.bfloat16), pltpu.VMEM((2, rows, HEAD), jnp.bfloat16),
                pltpu.VMEM((2, halo, HEAD), jnp.bfloat16), pltpu.VMEM((2, halo, HEAD), jnp.bfloat16),
                dma((2, halos)), dma((2, halos)), dma((2, chunks)), dma((2, chunks)), dma((chunks,)),
                dma((chunks,)), dma((2, chunks)),
            ],
            compiler_params=pltpu.CompilerParams(
                collective_id=1, has_side_effects=True, vmem_limit_bytes=VMEM_LIMIT),
            name="return_units",
        )(dkv, dhalo)
        return dq, grad_pairs

    placed = (P("seq", "head"), P("seq", "head"), P("seq", "head"), P(("seq", "head"), None),
              P(("seq", "head"), None), P(("seq", "head")), P(("seq", "head")))
    return jax.shard_map(on_device, mesh=mesh, in_specs=placed, out_specs=(P("seq", "head"), P("seq", "head")),
                         check_vma=False)
```

```python
import functools
import math

import jax
import jax.numpy as jnp
from jax import lax
from jax.experimental import pallas as pl
from jax.experimental.pallas import tpu as pltpu
from jax.sharding import PartitionSpec as P

HEAD = 128
BLOCK = 128
SPAN = 6
MESH = pl.DeviceIdType.MESH
CHUNK = 128
WINDOW = 3
BACK_WINDOW = 3
ARRIVE, RELAYED, LANDED = 3, 5, 7
BACK_RELAY, BACK_END = 3, 5
VMEM_LIMIT = 60 * 1024 * 1024
HOME = (0, 3)


def wait_for(ref, sem):
    pltpu.make_async_copy(ref, ref, sem).wait()


def kernel(ns, nh, rows, kv_ref, q_hbm, up_hbm, lo_ref, hi_ref, anc_ref, val_ref, dq_ref, dkv_ref,
           unit, kv, meta, meta_s, q_ref, up_ref, acc, back, halo_out, halo_in, part_buf, chain_buf,
           load_sem, meta_z_send, meta_z_recv, meta_y_send, meta_y_recv,
           right_send, left_send, chain_recv, y_send, kv_recv, halo_send, halo_recv,
           hback_send, hback_recv, yb_send, yb_recv, bleft_send, bright_send, bchain_recv):
    s, h = lax.axis_index("seq"), lax.axis_index("head")
    y, zh = h // 4, h % 4
    n = rows // CHUNK
    halo = SPAN * BLOCK
    nhalo = halo // CHUNK
    after, before = (s + 1) % ns, (s + ns - 1) % ns
    factor = HEAD ** -0.5
    scale = factor * math.log2(math.e)

    def peer(py, pz):
        return (s, py * 4 + pz)

    def when(cond):
        return pl.when(cond)

    mine = 2 * (((zh + 1) % 4) // 2) + zh // 3
    load = pltpu.make_async_copy(kv_ref, unit.at[mine], load_sem.at[0])
    load.start()
    load_q = pltpu.make_async_copy(q_hbm, q_ref, load_sem.at[1])
    load_up = pltpu.make_async_copy(up_hbm, up_ref, load_sem.at[2])

    barrier = pltpu.get_barrier_semaphore()
    for step in range(1, 4):
        pl.semaphore_signal(barrier, inc=1, device_id=peer((y + step) % 4, zh), device_id_type=MESH)
        pl.semaphore_signal(barrier, inc=1, device_id=peer(y, (zh + step) % 4), device_id_type=MESH)
    pl.semaphore_signal(barrier, inc=1, device_id=(after, h), device_id_type=MESH)
    pl.semaphore_signal(barrier, inc=1, device_id=(before, h), device_id_type=MESH)

    block = s * nh + h
    lane = lax.broadcasted_iota(jnp.int32, (1, BLOCK), 1)
    away = [jnp.where(val_ref[0, a] > 0, block - anc_ref[0, a], 0) for a in range(2)]
    meta[h, :, 0:BLOCK] = lo_ref[...]
    meta[h, :, BLOCK:2 * BLOCK] = hi_ref[...]
    meta[h, :, 2 * BLOCK:] = jnp.where(lane == 0, away[0], 0) + jnp.where(lane == 1, away[1], 0)
    load.wait()
    pl.semaphore_wait(barrier, 8)

    def part(c):
        start = c * CHUNK
        return pl.ds(start if isinstance(start, int) else pl.multiple_of(start, CHUNK), CHUNK)

    def chunk_at(k):
        return n - 1 - k

    def back_at(g):
        return (2 * n - 1 - nhalo - g) % n

    def remote(src, dst, send, recv, to):
        return pltpu.make_async_remote_copy(
            src_ref=src, dst_ref=dst, send_sem=send, recv_sem=recv, device_id=to, device_id_type=MESH)

    def meta_z(step):
        return remote(meta.at[h], meta.at[h], meta_z_send.at[step - 1], meta_z_recv.at[step - 1],
                      peer(y, (zh + step) % 4))

    def meta_y(step):
        rows4 = pl.ds(4 * y, 4)
        return remote(meta.at[rows4], meta.at[rows4], meta_y_send.at[step - 1], meta_y_recv.at[step - 1],
                      peer((y + step) % 4, zh))

    def right(c):
        return remote(unit.at[2 * (zh % 2), part(c)], unit.at[0, part(c)], right_send.at[c], chain_recv.at[0, c],
                      (s, (h + 1) % nh))

    def left(c):
        return remote(unit.at[2 - zh % 2, part(c)], unit.at[1, part(c)], left_send.at[c], chain_recv.at[1, c],
                      (s, (h + nh - 1) % nh))

    kind = y // 2

    def landing(which, c):
        return kv.at[which, part(c + nhalo)]

    def along_y(slot, c):
        return remote(unit.at[slot, part(c)], landing(kind, c), y_send.at[slot, c], kv_recv.at[kind, c],
                      peer(2 * (y % 2) + slot, zh))

    def stay(slot, c):
        return pltpu.make_async_copy(unit.at[slot, part(c)], landing(kind, c), kv_recv.at[kind, c])

    def to_next(which, piece):
        return remote(landing(which, piece + n - nhalo), kv.at[which, part(piece)], halo_send.at[which, piece],
                      halo_recv.at[which, piece], (after, h))

    def to_before(which, piece):
        return remote(halo_out.at[which, part(piece)], halo_in.at[which, part(piece)], hback_send.at[which, piece],
                      hback_recv.at[which, piece], (before, h))

    bslot = y % 2

    def back_y(which, c):
        return remote(back.at[which, part(c)], part_buf.at[bslot, part(c)], yb_send.at[which, c],
                      yb_recv.at[bslot, c], peer(2 * which + y // 2, zh))

    def back_stay(which, c):
        return pltpu.make_async_copy(back.at[which, part(c)], part_buf.at[bslot, part(c)], yb_recv.at[bslot, c])

    def back_left(c):
        return remote(part_buf.at[0, part(c)], chain_buf.at[0, part(c)], bleft_send.at[c], bchain_recv.at[0, c],
                      (s, (h + nh - 1) % nh))

    def back_right(c):
        return remote(part_buf.at[1, part(c)], chain_buf.at[1, part(c)], bright_send.at[c], bchain_recv.at[1, c],
                      (s, (h + 1) % nh))

    def own_start(k):
        @when(zh <= 1)
        def _():
            right(chunk_at(k)).start()

        @when(zh >= 2)
        def _():
            left(chunk_at(k)).start()

    def own_sent(k):
        @when(zh <= 1)
        def _():
            right(chunk_at(k)).wait_send()

        @when(zh >= 2)
        def _():
            left(chunk_at(k)).wait_send()

    for step in range(1, 4):
        meta_z(step).start()
    load_q.start()
    load_up.start()
    acc[...] = jnp.zeros_like(acc)

    key_at = lax.broadcasted_iota(jnp.int32, (BLOCK, BLOCK), 0)
    query_at = lax.broadcasted_iota(jnp.int32, (BLOCK, BLOCK), 1)
    nt = (((1,), (1,)), ((), ()))
    tn = (((0,), (0,)), ((), ()))

    def visit(i):
        def tile(d):
            return pl.ds(pl.multiple_of((i + SPAN - d) * BLOCK, BLOCK), BLOCK)

        mine_rows = pl.ds(pl.multiple_of(i * BLOCK, BLOCK), BLOCK)
        off = [meta_s[i, 0, 2 * BLOCK + a] for a in range(2)]
        q = jnp.concatenate([q_ref[mine_rows, :HEAD], q_ref[mine_rows, HEAD:]], axis=0)
        up = jnp.concatenate([up_ref[mine_rows, :HEAD], up_ref[mine_rows, HEAD:]], axis=0)

        def listed(which):
            picked = [jnp.zeros((BLOCK, HEAD), jnp.bfloat16) for _ in range(2)]
            for d in range(1, SPAN + 1):
                here = kv[which, tile(d), :]
                picked = [jnp.where(off[a] == d, here, picked[a]) for a in range(2)]
            return jnp.concatenate([kv[which, tile(0), :]] + picked, axis=0)

        k, v = listed(0), listed(1)
        scores = lax.dot_general(k, q, nt, preferred_element_type=jnp.float32)
        sens = lax.dot_general(v, up, nt, preferred_element_type=jnp.float32)
        lo_row = meta[i, :, 0:BLOCK].astype(jnp.float32)
        hi_row = meta[i, :, BLOCK:2 * BLOCK].astype(jnp.float32)
        hi_col = jnp.broadcast_to(hi_row, (BLOCK, BLOCK)).T
        seen = (key_at <= query_at) & (lo_row <= hi_col)
        seen = jnp.concatenate([seen, seen], axis=1)
        low = -jnp.inf
        scores = jnp.concatenate(
            [jnp.where(seen, scores[:BLOCK], low)]
            + [scores[BLOCK * (1 + a):BLOCK * (2 + a)] + jnp.where(off[a] > 0, 0.0, low) for a in range(2)], axis=0)
        top = jnp.max(scores, axis=0, keepdims=True)
        exps = jnp.exp2((scores - top) * scale)
        inverse = 1.0 / jnp.sum(exps, axis=0, keepdims=True)
        probs = exps * inverse
        delta = jnp.sum(probs * sens, axis=0, keepdims=True)
        weights = probs.astype(jnp.bfloat16)
        slopes = (probs * (sens - delta)).astype(jnp.bfloat16)
        dq = lax.dot_general(slopes, k, tn, preferred_element_type=jnp.float32) * factor
        dq_ref[mine_rows, :HEAD] = dq[:BLOCK].astype(jnp.bfloat16)
        dq_ref[mine_rows, HEAD:] = dq[BLOCK:].astype(jnp.bfloat16)
        for which, (left_side, right_side) in enumerate(((slopes, q), (weights, up))):
            grad = jnp.dot(left_side, right_side, preferred_element_type=jnp.float32)
            acc[which, tile(0), :] += grad[:BLOCK]
            for d in range(1, SPAN + 1):
                term = jnp.where(off[1] == d, grad[2 * BLOCK:], 0.0)
                term = jnp.where(off[0] == d, grad[BLOCK:2 * BLOCK], term)
                acc[which, tile(d), :] += term

    def total(slot, c):
        return (part_buf[slot, part(c)].astype(jnp.float32)
                + chain_buf[slot, part(c)].astype(jnp.float32)).astype(jnp.bfloat16)

    def bown_start(g):
        j = back_at(g)

        @when(zh % 2 == 1)
        def _():
            back_left(j).start()

        @when(zh % 2 == 0)
        def _():
            back_right(j).start()

    def bown_sent(g):
        j = back_at(g)

        @when(zh % 2 == 1)
        def _():
            back_left(j).wait_send()

        @when(zh % 2 == 0)
        def _():
            back_right(j).wait_send()

    first_compute = nhalo + LANDED
    last_compute = first_compute + n - 1
    first_give = first_compute + nhalo
    first_back = first_give + 2
    backs = (last_compute - first_back) // 2 + 1
    steps = last_compute + 1 + n + BACK_END - backs

    def step(t, carry):
        @when((t >= WINDOW) & (t < n + WINDOW))
        def _():
            own_sent(t - WINDOW)

        @when(t < n)
        def _():
            own_start(t)

        for slot in range(2):
            k = t - jnp.where(zh == 3 - 3 * slot, RELAYED, ARRIVE)

            @when((k >= 0) & (k < n))
            def _():
                c = chunk_at(k)

                @when(zh != 3 * slot)
                def _():
                    wait_for(unit.at[slot, part(c)], chain_recv.at[slot, c])

                @when(zh == 2 - slot)
                def _():
                    (right if slot == 0 else left)(c).start()

                @when(y == HOME[slot])
                def _():
                    stay(slot, c).start()

                @when(y != HOME[slot])
                def _():
                    along_y(slot, c).start()

        u = jnp.where(t > last_compute, backs + t - last_compute - 1, (t - first_back) // 2)
        turn = (t > last_compute) | ((t >= first_back) & ((t - first_back) % 2 == 0))

        @when(t == 2)
        def _():
            for i in range(1, 4):
                wait_for(meta.at[y * 4 + (zh + 4 - i) % 4], meta_z_recv.at[i - 1])
            for i in range(1, 4):
                meta_y(i).start()

        @when(turn & (u >= BACK_WINDOW) & (u < n + BACK_WINDOW))
        def _():
            bown_sent(u - BACK_WINDOW)

        @when(turn & (u < n))
        def _():
            j = back_at(u)
            for slot in range(2):
                wait_for(part_buf.at[slot, part(j)], yb_recv.at[slot, j])
            bown_start(u)

        @when((t >= LANDED) & (t < n + LANDED))
        def _():
            k = t - LANDED
            c = chunk_at(k)
            for which in range(2):
                wait_for(landing(which, c), kv_recv.at[which, c])

            @when(k < nhalo)
            def _():
                for which in range(2):
                    to_next(which, nhalo - 1 - k).start()

        @when(t == first_compute)
        def _():
            for i in range(1, 4):
                wait_for(meta.at[pl.ds(4 * ((y + 4 - i) % 4), 4)], meta_y_recv.at[i - 1])
            copy = pltpu.make_async_copy(meta, meta_s, load_sem.at[3])
            copy.start()
            load_q.wait()
            load_up.wait()
            copy.wait()

        @when((t >= first_compute) & (t <= last_compute))
        def _():
            i = last_compute - t

            @when(i < nhalo)
            def _():
                for which in range(2):
                    wait_for(kv.at[which, part(i)], halo_recv.at[which, i])

            for b in range(CHUNK // BLOCK):
                visit(i * (CHUNK // BLOCK) + b)

        @when(t == last_compute)
        def _():
            for piece in range(nhalo)[::-1]:
                for which in range(2):
                    scaled = acc[which, part(piece)] * (factor if which == 0 else 1.0)
                    halo_out[which, part(piece)] = scaled.astype(jnp.bfloat16)
                    to_before(which, piece).start()

        @when(turn & (u >= BACK_RELAY) & (u < n + BACK_RELAY))
        def _():
            j = back_at(u - BACK_RELAY)

            @when(zh == 2)
            def _():
                wait_for(chain_buf.at[0, part(j)], bchain_recv.at[0, j])
                part_buf[0, part(j)] = total(0, j)
                back_left(j).start()

            @when(zh == 1)
            def _():
                wait_for(chain_buf.at[1, part(j)], bchain_recv.at[1, j])
                part_buf[1, part(j)] = total(1, j)
                back_right(j).start()

        gives_early = (t >= first_give) & (t < first_give + n - nhalo)
        gives_late = turn & (u + 2 >= n - nhalo) & (u + 2 < n)

        @when(gives_early | gives_late)
        def _():
            j = back_at(jnp.where(gives_late, u + 2, t - first_give))
            for which in range(2):
                scaled = acc[which, part(j + nhalo)] * (factor if which == 0 else 1.0)

                @when(j < n - nhalo)
                def _():
                    back[which, part(j)] = scaled.astype(jnp.bfloat16)

                @when(j >= n - nhalo)
                def _():
                    piece = j - (n - nhalo)
                    wait_for(halo_in.at[which, part(piece)], hback_recv.at[which, piece])
                    back[which, part(j)] = (
                        scaled + halo_in[which, part(piece)].astype(jnp.float32)).astype(jnp.bfloat16)

                @when(y == HOME[which])
                def _():
                    back_stay(which, j).start()

                @when(y != HOME[which])
                def _():
                    back_y(which, j).start()

        @when(turn & (u >= BACK_END))
        def _():
            j = back_at(u - BACK_END)

            @when(zh <= 1)
            def _():
                wait_for(chain_buf.at[0, part(j)], bchain_recv.at[0, j])

            @when(zh >= 2)
            def _():
                wait_for(chain_buf.at[1, part(j)], bchain_recv.at[1, j])

            @when(zh == 0)
            def _():
                dkv_ref[part(j)] = total(0, j)

            @when(zh == 1)
            def _():
                dkv_ref[part(j)] = chain_buf[0, part(j)]

            @when(zh == 2)
            def _():
                dkv_ref[part(j)] = chain_buf[1, part(j)]

            @when(zh == 3)
            def _():
                dkv_ref[part(j)] = total(1, j)

        return carry

    lax.fori_loop(0, steps, step, 0)

    for i in range(1, 4):
        meta_z(i).wait_send()
        meta_y(i).wait_send()

    def drain(k, carry):
        @when(zh == 2)
        def _():
            right(k).wait_send()
            back_left(k).wait_send()

        @when(zh == 1)
        def _():
            left(k).wait_send()
            back_right(k).wait_send()

        for slot in range(2):
            @when(y != HOME[slot])
            def _():
                along_y(slot, k).wait_send()
                back_y(slot, k).wait_send()

            @when(k < nhalo)
            def _():
                to_next(slot, k).wait_send()
                to_before(slot, k).wait_send()

        return carry

    lax.fori_loop(0, n, drain, 0)


def solution(mesh):
    ns, nh = mesh.shape["seq"], mesh.shape["head"]

    def on_device(queries, key_value_rows, upstream, ancestors, valid, span_lo, span_hi):
        rows = queries.shape[0]
        halo = SPAN * BLOCK
        n, nhalo = rows // CHUNK, halo // CHUNK
        hbm = pl.BlockSpec(memory_space=pl.ANY)
        vmem = pl.BlockSpec(memory_space=pltpu.VMEM)
        smem = pl.BlockSpec(memory_space=pltpu.SMEM)
        dma = pltpu.SemaphoreType.DMA
        bf16, f32 = jnp.bfloat16, jnp.float32
        return pl.pallas_call(
            functools.partial(kernel, ns, nh, rows),
            out_shape=(jax.ShapeDtypeStruct(queries.shape, bf16), jax.ShapeDtypeStruct((rows, HEAD), bf16)),
            in_specs=[hbm, hbm, hbm, vmem, vmem, smem, smem],
            out_specs=(vmem, vmem),
            scratch_shapes=[
                pltpu.VMEM((3, rows, HEAD), bf16), pltpu.VMEM((2, halo + rows, HEAD), bf16),
                pltpu.VMEM((nh, 1, 3 * BLOCK), jnp.int32), pltpu.SMEM((nh, 1, 3 * BLOCK), jnp.int32),
                pltpu.VMEM(queries.shape, bf16), pltpu.VMEM(queries.shape, bf16),
                pltpu.VMEM((2, halo + rows, HEAD), f32), pltpu.VMEM((2, rows, HEAD), bf16),
                pltpu.VMEM((2, halo, HEAD), bf16), pltpu.VMEM((2, halo, HEAD), bf16),
                pltpu.VMEM((2, rows, HEAD), bf16), pltpu.VMEM((2, rows, HEAD), bf16),
                dma((4,)), dma((3,)), dma((3,)), dma((3,)), dma((3,)),
                dma((n,)), dma((n,)), dma((2, n)), dma((2, n)), dma((2, n)), dma((2, nhalo)), dma((2, nhalo)),
                dma((2, nhalo)), dma((2, nhalo)), dma((2, n)), dma((2, n)), dma((n,)), dma((n,)), dma((2, n)),
            ],
            compiler_params=pltpu.CompilerParams(
                collective_id=0, has_side_effects=True, vmem_limit_bytes=VMEM_LIMIT),
            name="tree_attention",
        )(key_value_rows, queries, upstream, span_lo.reshape(1, BLOCK), span_hi.reshape(1, BLOCK), ancestors, valid)

    placed = (P("seq", "head"), P("seq", "head"), P("seq", "head"), P(("seq", "head"), None),
              P(("seq", "head"), None), P(("seq", "head")), P(("seq", "head")))
    return jax.shard_map(on_device, mesh=mesh, in_specs=placed, out_specs=(P("seq", "head"), P("seq", "head")),
                         check_vma=False)
```

```python
import functools
import math

import jax
import jax.numpy as jnp
from jax import lax
from jax.experimental import pallas as pl
from jax.experimental.pallas import tpu as pltpu
from jax.sharding import PartitionSpec as P

HEAD = 128
BLOCK = 128
SPAN = 6
MESH = pl.DeviceIdType.MESH
CHUNK = 256
WINDOW = 2
BACK_WINDOW = 3
ARRIVE, RELAYED, LANDED = 2, 3, 4
BACK_RELAY, BACK_END = 2, 4
VMEM_LIMIT = 60 * 1024 * 1024
HOME = (0, 3)


def wait_for(ref, sem):
    pltpu.make_async_copy(ref, ref, sem).wait()


def kernel(ns, nh, rows, kv_ref, q_hbm, up_hbm, lo_ref, hi_ref, anc_ref, val_ref, dq_ref, dkv_ref,
           unit, kv, meta, meta_s, q_ref, up_ref, acc, back, halo_out, halo_in, part_buf, chain_buf,
           load_sem, meta_z_send, meta_z_recv, meta_y_send, meta_y_recv,
           right_send, left_send, chain_recv, y_send, kv_recv, halo_send, halo_recv,
           hback_send, hback_recv, yb_send, yb_recv, bleft_send, bright_send, bchain_recv):
    s, h = lax.axis_index("seq"), lax.axis_index("head")
    y, zh = h // 4, h % 4
    n = rows // CHUNK
    halo = SPAN * BLOCK
    nhalo = halo // CHUNK
    after, before = (s + 1) % ns, (s + ns - 1) % ns
    factor = HEAD ** -0.5
    scale = factor * math.log2(math.e)

    def peer(py, pz):
        return (s, py * 4 + pz)

    def when(cond):
        return pl.when(cond)

    mine = 2 * (((zh + 1) % 4) // 2) + zh // 3
    load = pltpu.make_async_copy(kv_ref, unit.at[mine], load_sem.at[0])
    load.start()
    load_q = pltpu.make_async_copy(q_hbm, q_ref, load_sem.at[1])
    load_up = pltpu.make_async_copy(up_hbm, up_ref, load_sem.at[2])

    barrier = pltpu.get_barrier_semaphore()
    for step in range(1, 4):
        pl.semaphore_signal(barrier, inc=1, device_id=peer((y + step) % 4, zh), device_id_type=MESH)
        pl.semaphore_signal(barrier, inc=1, device_id=peer(y, (zh + step) % 4), device_id_type=MESH)
    pl.semaphore_signal(barrier, inc=1, device_id=(after, h), device_id_type=MESH)
    pl.semaphore_signal(barrier, inc=1, device_id=(before, h), device_id_type=MESH)

    block = s * nh + h
    lane = lax.broadcasted_iota(jnp.int32, (1, BLOCK), 1)
    away = [jnp.where(val_ref[0, a] > 0, block - anc_ref[0, a], 0) for a in range(2)]
    meta[h, :, 0:BLOCK] = lo_ref[...]
    meta[h, :, BLOCK:2 * BLOCK] = hi_ref[...]
    meta[h, :, 2 * BLOCK:] = jnp.where(lane == 0, away[0], 0) + jnp.where(lane == 1, away[1], 0)
    load.wait()
    pl.semaphore_wait(barrier, 8)

    def part(c):
        start = c * CHUNK
        return pl.ds(start if isinstance(start, int) else pl.multiple_of(start, CHUNK), CHUNK)

    def chunk_at(k):
        return n - 1 - k

    def back_at(g):
        return (2 * n - 1 - nhalo - g) % n

    def remote(src, dst, send, recv, to):
        return pltpu.make_async_remote_copy(
            src_ref=src, dst_ref=dst, send_sem=send, recv_sem=recv, device_id=to, device_id_type=MESH)

    def meta_z(step):
        return remote(meta.at[h], meta.at[h], meta_z_send.at[step - 1], meta_z_recv.at[step - 1],
                      peer(y, (zh + step) % 4))

    def meta_y(step):
        rows4 = pl.ds(4 * y, 4)
        return remote(meta.at[rows4], meta.at[rows4], meta_y_send.at[step - 1], meta_y_recv.at[step - 1],
                      peer((y + step) % 4, zh))

    def right(c):
        return remote(unit.at[2 * (zh % 2), part(c)], unit.at[0, part(c)], right_send.at[c], chain_recv.at[0, c],
                      (s, (h + 1) % nh))

    def left(c):
        return remote(unit.at[2 - zh % 2, part(c)], unit.at[1, part(c)], left_send.at[c], chain_recv.at[1, c],
                      (s, (h + nh - 1) % nh))

    kind = y // 2

    def landing(which, c):
        return kv.at[which, part(c + nhalo)]

    def along_y(slot, c):
        return remote(unit.at[slot, part(c)], landing(kind, c), y_send.at[slot, c], kv_recv.at[kind, c],
                      peer(2 * (y % 2) + slot, zh))

    def stay(slot, c):
        return pltpu.make_async_copy(unit.at[slot, part(c)], landing(kind, c), kv_recv.at[kind, c])

    def to_next(piece):
        return remote(kv.at[:, part(piece + n)], kv.at[:, part(piece)], halo_send.at[piece], halo_recv.at[piece],
                      (after, h))

    def to_before(piece):
        return remote(halo_out.at[:, part(piece)], halo_in.at[:, part(piece)], hback_send.at[piece],
                      hback_recv.at[piece], (before, h))

    bslot = y % 2

    def back_y(which, c):
        return remote(back.at[which, part(c)], part_buf.at[bslot, part(c)], yb_send.at[which, c],
                      yb_recv.at[bslot, c], peer(2 * which + y // 2, zh))

    def back_stay(which, c):
        return pltpu.make_async_copy(back.at[which, part(c)], part_buf.at[bslot, part(c)], yb_recv.at[bslot, c])

    def back_left(c):
        return remote(part_buf.at[0, part(c)], chain_buf.at[0, part(c)], bleft_send.at[c], bchain_recv.at[0, c],
                      (s, (h + nh - 1) % nh))

    def back_right(c):
        return remote(part_buf.at[1, part(c)], chain_buf.at[1, part(c)], bright_send.at[c], bchain_recv.at[1, c],
                      (s, (h + 1) % nh))

    def own_start(k):
        @when(zh <= 1)
        def _():
            right(chunk_at(k)).start()

        @when(zh >= 2)
        def _():
            left(chunk_at(k)).start()

    def own_sent(k):
        @when(zh <= 1)
        def _():
            right(chunk_at(k)).wait_send()

        @when(zh >= 2)
        def _():
            left(chunk_at(k)).wait_send()

    for step in range(1, 4):
        meta_z(step).start()
    load_q.start()
    load_up.start()
    acc[...] = jnp.zeros_like(acc)

    key_at = lax.broadcasted_iota(jnp.int32, (BLOCK, BLOCK), 0)
    query_at = lax.broadcasted_iota(jnp.int32, (BLOCK, BLOCK), 1)
    nt = (((1,), (1,)), ((), ()))
    tn = (((0,), (0,)), ((), ()))

    def visit(i):
        def tile(d):
            return pl.ds(pl.multiple_of((i + SPAN - d) * BLOCK, BLOCK), BLOCK)

        mine_rows = pl.ds(pl.multiple_of(i * BLOCK, BLOCK), BLOCK)
        off = [meta_s[i, 0, 2 * BLOCK + a] for a in range(2)]
        q = jnp.concatenate([q_ref[mine_rows, :HEAD], q_ref[mine_rows, HEAD:]], axis=0)
        up = jnp.concatenate([up_ref[mine_rows, :HEAD], up_ref[mine_rows, HEAD:]], axis=0)

        def listed(which):
            picked = [jnp.zeros((BLOCK, HEAD), jnp.bfloat16) for _ in range(2)]
            for d in range(1, SPAN + 1):
                here = kv[which, tile(d), :]
                picked = [jnp.where(off[a] == d, here, picked[a]) for a in range(2)]
            return jnp.concatenate([kv[which, tile(0), :]] + picked, axis=0)

        k, v = listed(0), listed(1)
        scores = lax.dot_general(k, q, nt, preferred_element_type=jnp.float32)
        sens = lax.dot_general(v, up, nt, preferred_element_type=jnp.float32)
        lo_row = meta[i, :, 0:BLOCK].astype(jnp.float32)
        hi_row = meta[i, :, BLOCK:2 * BLOCK].astype(jnp.float32)
        hi_col = jnp.broadcast_to(hi_row, (BLOCK, BLOCK)).T
        seen = (key_at <= query_at) & (lo_row <= hi_col)
        seen = jnp.concatenate([seen, seen], axis=1)
        low = -jnp.inf
        scores = jnp.concatenate(
            [jnp.where(seen, scores[:BLOCK], low)]
            + [scores[BLOCK * (1 + a):BLOCK * (2 + a)] + jnp.where(off[a] > 0, 0.0, low) for a in range(2)], axis=0)
        top = jnp.max(scores, axis=0, keepdims=True)
        exps = jnp.exp2((scores - top) * scale)
        inverse = 1.0 / jnp.sum(exps, axis=0, keepdims=True)
        probs = exps * inverse
        delta = jnp.sum(probs * sens, axis=0, keepdims=True)
        weights = probs.astype(jnp.bfloat16)
        slopes = (probs * (sens - delta)).astype(jnp.bfloat16)
        dq = lax.dot_general(slopes, k, tn, preferred_element_type=jnp.float32) * factor
        dq_ref[mine_rows, :HEAD] = dq[:BLOCK].astype(jnp.bfloat16)
        dq_ref[mine_rows, HEAD:] = dq[BLOCK:].astype(jnp.bfloat16)
        for which, (left_side, right_side) in enumerate(((slopes, q), (weights, up))):
            grad = jnp.dot(left_side, right_side, preferred_element_type=jnp.float32)
            acc[which, tile(0), :] += grad[:BLOCK]
            for d in range(1, SPAN + 1):
                term = jnp.where(off[1] == d, grad[2 * BLOCK:], 0.0)
                term = jnp.where(off[0] == d, grad[BLOCK:2 * BLOCK], term)
                acc[which, tile(d), :] += term

    def total(slot, c):
        return (part_buf[slot, part(c)].astype(jnp.float32)
                + chain_buf[slot, part(c)].astype(jnp.float32)).astype(jnp.bfloat16)

    def bown_start(g):
        j = back_at(g)

        @when(zh % 2 == 1)
        def _():
            back_left(j).start()

        @when(zh % 2 == 0)
        def _():
            back_right(j).start()

    def bown_sent(g):
        j = back_at(g)

        @when(zh % 2 == 1)
        def _():
            back_left(j).wait_send()

        @when(zh % 2 == 0)
        def _():
            back_right(j).wait_send()

    first_compute = nhalo + LANDED
    last_compute = first_compute + n - 1
    first_give = first_compute + nhalo
    first_back = first_give + 2
    backs = (last_compute - first_back) // 2 + 1
    steps = last_compute + 1 + n + BACK_END - backs

    def step(t, carry):
        @when((t >= WINDOW) & (t < n + WINDOW))
        def _():
            own_sent(t - WINDOW)

        @when(t < n)
        def _():
            own_start(t)

        for slot in range(2):
            k = t - jnp.where(zh == 3 - 3 * slot, RELAYED, ARRIVE)

            @when((k >= 0) & (k < n))
            def _():
                c = chunk_at(k)

                @when(zh != 3 * slot)
                def _():
                    wait_for(unit.at[slot, part(c)], chain_recv.at[slot, c])

                @when(zh == 2 - slot)
                def _():
                    (right if slot == 0 else left)(c).start()

                @when(y == HOME[slot])
                def _():
                    stay(slot, c).start()

                @when(y != HOME[slot])
                def _():
                    along_y(slot, c).start()

        u = jnp.where(t > last_compute, backs + t - last_compute - 1, (t - first_back) // 2)
        turn = (t > last_compute) | ((t >= first_back) & ((t - first_back) % 2 == 0))

        @when(t == 2)
        def _():
            for i in range(1, 4):
                wait_for(meta.at[y * 4 + (zh + 4 - i) % 4], meta_z_recv.at[i - 1])
            for i in range(1, 4):
                meta_y(i).start()

        @when(turn & (u >= BACK_WINDOW) & (u < n + BACK_WINDOW))
        def _():
            bown_sent(u - BACK_WINDOW)

        @when(turn & (u < n))
        def _():
            j = back_at(u)
            for slot in range(2):
                wait_for(part_buf.at[slot, part(j)], yb_recv.at[slot, j])
            bown_start(u)

        @when((t >= LANDED) & (t < n + LANDED))
        def _():
            k = t - LANDED
            c = chunk_at(k)
            for which in range(2):
                wait_for(landing(which, c), kv_recv.at[which, c])

            @when(k < nhalo)
            def _():
                to_next(nhalo - 1 - k).start()

        @when(t == first_compute)
        def _():
            for i in range(1, 4):
                wait_for(meta.at[pl.ds(4 * ((y + 4 - i) % 4), 4)], meta_y_recv.at[i - 1])
            copy = pltpu.make_async_copy(meta, meta_s, load_sem.at[3])
            copy.start()
            load_q.wait()
            load_up.wait()
            copy.wait()

        @when((t >= first_compute) & (t <= last_compute))
        def _():
            i = last_compute - t

            @when(i < nhalo)
            def _():
                wait_for(kv.at[:, part(i)], halo_recv.at[i])

            for b in range(CHUNK // BLOCK):
                visit(i * (CHUNK // BLOCK) + b)

        @when(t == last_compute)
        def _():
            for piece in range(nhalo)[::-1]:
                for which in range(2):
                    scaled = acc[which, part(piece)] * (factor if which == 0 else 1.0)
                    halo_out[which, part(piece)] = scaled.astype(jnp.bfloat16)
                to_before(piece).start()

        @when(turn & (u >= BACK_RELAY) & (u < n + BACK_RELAY))
        def _():
            j = back_at(u - BACK_RELAY)

            @when(zh == 2)
            def _():
                wait_for(chain_buf.at[0, part(j)], bchain_recv.at[0, j])
                part_buf[0, part(j)] = total(0, j)
                back_left(j).start()

            @when(zh == 1)
            def _():
                wait_for(chain_buf.at[1, part(j)], bchain_recv.at[1, j])
                part_buf[1, part(j)] = total(1, j)
                back_right(j).start()

        gives_early = (t >= first_give) & (t < first_give + n - nhalo)
        gives_late = turn & (u + 2 >= n - nhalo) & (u + 2 < n)

        @when(gives_early | gives_late)
        def _():
            j = back_at(jnp.where(gives_late, u + 2, t - first_give))

            @when(j >= n - nhalo)
            def _():
                piece = j - (n - nhalo)
                wait_for(halo_in.at[:, part(piece)], hback_recv.at[piece])

            for which in range(2):
                scaled = acc[which, part(j + nhalo)] * (factor if which == 0 else 1.0)

                @when(j < n - nhalo)
                def _():
                    back[which, part(j)] = scaled.astype(jnp.bfloat16)

                @when(j >= n - nhalo)
                def _():
                    piece = j - (n - nhalo)
                    back[which, part(j)] = (
                        scaled + halo_in[which, part(piece)].astype(jnp.float32)).astype(jnp.bfloat16)

                @when(y == HOME[which])
                def _():
                    back_stay(which, j).start()

                @when(y != HOME[which])
                def _():
                    back_y(which, j).start()

        @when(turn & (u >= BACK_END))
        def _():
            j = back_at(u - BACK_END)

            @when(zh <= 1)
            def _():
                wait_for(chain_buf.at[0, part(j)], bchain_recv.at[0, j])

            @when(zh >= 2)
            def _():
                wait_for(chain_buf.at[1, part(j)], bchain_recv.at[1, j])

            @when(zh == 0)
            def _():
                dkv_ref[part(j)] = total(0, j)

            @when(zh == 1)
            def _():
                dkv_ref[part(j)] = chain_buf[0, part(j)]

            @when(zh == 2)
            def _():
                dkv_ref[part(j)] = chain_buf[1, part(j)]

            @when(zh == 3)
            def _():
                dkv_ref[part(j)] = total(1, j)

        return carry

    lax.fori_loop(0, steps, step, 0)

    for i in range(1, 4):
        meta_z(i).wait_send()
        meta_y(i).wait_send()

    def drain(k, carry):
        @when(zh == 2)
        def _():
            right(k).wait_send()
            back_left(k).wait_send()

        @when(zh == 1)
        def _():
            left(k).wait_send()
            back_right(k).wait_send()

        for slot in range(2):
            @when(y != HOME[slot])
            def _():
                along_y(slot, k).wait_send()
                back_y(slot, k).wait_send()

        @when(k < nhalo)
        def _():
            to_next(k).wait_send()
            to_before(k).wait_send()

        return carry

    lax.fori_loop(0, n, drain, 0)


def solution(mesh):
    ns, nh = mesh.shape["seq"], mesh.shape["head"]

    def on_device(queries, key_value_rows, upstream, ancestors, valid, span_lo, span_hi):
        rows = queries.shape[0]
        halo = SPAN * BLOCK
        n, nhalo = rows // CHUNK, halo // CHUNK
        hbm = pl.BlockSpec(memory_space=pl.ANY)
        vmem = pl.BlockSpec(memory_space=pltpu.VMEM)
        smem = pl.BlockSpec(memory_space=pltpu.SMEM)
        dma = pltpu.SemaphoreType.DMA
        bf16, f32 = jnp.bfloat16, jnp.float32
        return pl.pallas_call(
            functools.partial(kernel, ns, nh, rows),
            out_shape=(jax.ShapeDtypeStruct(queries.shape, bf16), jax.ShapeDtypeStruct((rows, HEAD), bf16)),
            in_specs=[hbm, hbm, hbm, vmem, vmem, smem, smem],
            out_specs=(vmem, vmem),
            scratch_shapes=[
                pltpu.VMEM((3, rows, HEAD), bf16), pltpu.VMEM((2, halo + rows, HEAD), bf16),
                pltpu.VMEM((nh, 1, 3 * BLOCK), jnp.int32), pltpu.SMEM((nh, 1, 3 * BLOCK), jnp.int32),
                pltpu.VMEM(queries.shape, bf16), pltpu.VMEM(queries.shape, bf16),
                pltpu.VMEM((2, halo + rows, HEAD), f32), pltpu.VMEM((2, rows, HEAD), bf16),
                pltpu.VMEM((2, halo, HEAD), bf16), pltpu.VMEM((2, halo, HEAD), bf16),
                pltpu.VMEM((2, rows, HEAD), bf16), pltpu.VMEM((2, rows, HEAD), bf16),
                dma((4,)), dma((3,)), dma((3,)), dma((3,)), dma((3,)),
                dma((n,)), dma((n,)), dma((2, n)), dma((2, n)), dma((2, n)), dma((nhalo,)), dma((nhalo,)),
                dma((nhalo,)), dma((nhalo,)), dma((2, n)), dma((2, n)), dma((n,)), dma((n,)), dma((2, n)),
            ],
            compiler_params=pltpu.CompilerParams(
                collective_id=0, has_side_effects=True, vmem_limit_bytes=VMEM_LIMIT),
            name="tree_attention",
        )(key_value_rows, queries, upstream, span_lo.reshape(1, BLOCK), span_hi.reshape(1, BLOCK), ancestors, valid)

    placed = (P("seq", "head"), P("seq", "head"), P("seq", "head"), P(("seq", "head"), None),
              P(("seq", "head"), None), P(("seq", "head")), P(("seq", "head")))
    return jax.shard_map(on_device, mesh=mesh, in_specs=placed, out_specs=(P("seq", "head"), P("seq", "head")),
                         check_vma=False)
```

```python
import functools
import math

import jax
import jax.numpy as jnp
from jax import lax
from jax.experimental import pallas as pl
from jax.experimental.pallas import tpu as pltpu
from jax.sharding import PartitionSpec as P

HEAD = 128
BLOCK = 128
SPAN = 6
MESH = pl.DeviceIdType.MESH
CHUNK = 256
WINDOW = 2
BACK_WINDOW = 3
ARRIVE, RELAYED, LANDED = 2, 3, 4
BACK_RELAY, BACK_END = 2, 4
VMEM_LIMIT = 60 * 1024 * 1024
HOME = (0, 3)


def wait_for(ref, sem):
    pltpu.make_async_copy(ref, ref, sem).wait()


def kernel(ns, nh, rows, kv_ref, q_hbm, up_hbm, lo_ref, hi_ref, anc_ref, val_ref, dq_ref, dkv_ref,
           unit, kv, meta, meta_s, q_ref, up_ref, acc, back, halo_out, halo_in, part_buf, chain_buf,
           load_sem, meta_z_send, meta_z_recv, meta_y_send, meta_y_recv,
           right_send, left_send, chain_recv, y_send, kv_recv, halo_send, halo_recv,
           hback_send, hback_recv, yb_send, yb_recv, bleft_send, bright_send, bchain_recv):
    s, h = lax.axis_index("seq"), lax.axis_index("head")
    y, zh = h // 4, h % 4
    n = rows // CHUNK
    halo = SPAN * BLOCK
    nhalo = halo // CHUNK
    after, before = (s + 1) % ns, (s + ns - 1) % ns
    factor = HEAD ** -0.5
    scale = factor * math.log2(math.e)

    def peer(py, pz):
        return (s, py * 4 + pz)

    def when(cond):
        return pl.when(cond)

    mine = 2 * (((zh + 1) % 4) // 2) + zh // 3
    load = pltpu.make_async_copy(kv_ref, unit.at[mine], load_sem.at[0])
    load.start()
    load_q = pltpu.make_async_copy(q_hbm, q_ref, load_sem.at[1])
    load_up = pltpu.make_async_copy(up_hbm, up_ref, load_sem.at[2])

    barrier = pltpu.get_barrier_semaphore()
    for step in range(1, 4):
        pl.semaphore_signal(barrier, inc=1, device_id=peer((y + step) % 4, zh), device_id_type=MESH)
        pl.semaphore_signal(barrier, inc=1, device_id=peer(y, (zh + step) % 4), device_id_type=MESH)
    pl.semaphore_signal(barrier, inc=1, device_id=(after, h), device_id_type=MESH)
    pl.semaphore_signal(barrier, inc=1, device_id=(before, h), device_id_type=MESH)

    block = s * nh + h
    lane = lax.broadcasted_iota(jnp.int32, (1, BLOCK), 1)
    away = [jnp.where(val_ref[0, a] > 0, block - anc_ref[0, a], 0) for a in range(2)]
    meta[h, :, 0:BLOCK] = lo_ref[...]
    meta[h, :, BLOCK:2 * BLOCK] = hi_ref[...]
    meta[h, :, 2 * BLOCK:] = jnp.where(lane == 0, away[0], 0) + jnp.where(lane == 1, away[1], 0)
    load.wait()
    pl.semaphore_wait(barrier, 8)

    def part(c):
        start = c * CHUNK
        return pl.ds(start if isinstance(start, int) else pl.multiple_of(start, CHUNK), CHUNK)

    def chunk_at(k):
        return n - 1 - k

    def back_at(g):
        return (2 * n - 1 - nhalo - g) % n

    def remote(src, dst, send, recv, to):
        return pltpu.make_async_remote_copy(
            src_ref=src, dst_ref=dst, send_sem=send, recv_sem=recv, device_id=to, device_id_type=MESH)

    def meta_z(step):
        return remote(meta.at[h], meta.at[h], meta_z_send.at[step - 1], meta_z_recv.at[step - 1],
                      peer(y, (zh + step) % 4))

    def meta_y(step):
        rows4 = pl.ds(4 * y, 4)
        return remote(meta.at[rows4], meta.at[rows4], meta_y_send.at[step - 1], meta_y_recv.at[step - 1],
                      peer((y + step) % 4, zh))

    def right(c):
        return remote(unit.at[2 * (zh % 2), part(c)], unit.at[0, part(c)], right_send.at[c], chain_recv.at[0, c],
                      (s, (h + 1) % nh))

    def left(c):
        return remote(unit.at[2 - zh % 2, part(c)], unit.at[1, part(c)], left_send.at[c], chain_recv.at[1, c],
                      (s, (h + nh - 1) % nh))

    kind = y // 2

    def landing(which, c):
        return kv.at[which, part(c + nhalo)]

    def along_y(slot, c):
        return remote(unit.at[slot, part(c)], landing(kind, c), y_send.at[slot, c], kv_recv.at[kind, c],
                      peer(2 * (y % 2) + slot, zh))

    def stay(slot, c):
        return pltpu.make_async_copy(unit.at[slot, part(c)], landing(kind, c), kv_recv.at[kind, c])

    def to_next(piece):
        return remote(kv.at[:, part(piece + n)], kv.at[:, part(piece)], halo_send.at[piece], halo_recv.at[piece],
                      (after, h))

    def to_before(piece):
        return remote(halo_out.at[:, part(piece)], halo_in.at[:, part(piece)], hback_send.at[piece],
                      hback_recv.at[piece], (before, h))

    bslot = y % 2

    def back_y(which, c):
        return remote(back.at[which, part(c)], part_buf.at[bslot, part(c)], yb_send.at[which, c],
                      yb_recv.at[bslot, c], peer(2 * which + y // 2, zh))

    def back_stay(which, c):
        return pltpu.make_async_copy(back.at[which, part(c)], part_buf.at[bslot, part(c)], yb_recv.at[bslot, c])

    def back_left(c):
        return remote(part_buf.at[0, part(c)], chain_buf.at[0, part(c)], bleft_send.at[c], bchain_recv.at[0, c],
                      (s, (h + nh - 1) % nh))

    def back_right(c):
        return remote(part_buf.at[1, part(c)], chain_buf.at[1, part(c)], bright_send.at[c], bchain_recv.at[1, c],
                      (s, (h + 1) % nh))

    def own_start(k):
        @when(zh <= 1)
        def _():
            right(chunk_at(k)).start()

        @when(zh >= 2)
        def _():
            left(chunk_at(k)).start()

    def own_sent(k):
        @when(zh <= 1)
        def _():
            right(chunk_at(k)).wait_send()

        @when(zh >= 2)
        def _():
            left(chunk_at(k)).wait_send()

    for step in range(1, 4):
        meta_z(step).start()
    load_q.start()
    load_up.start()
    acc[...] = jnp.zeros_like(acc)

    key_at = lax.broadcasted_iota(jnp.int32, (BLOCK, BLOCK), 0)
    query_at = lax.broadcasted_iota(jnp.int32, (BLOCK, BLOCK), 1)
    nt = (((1,), (1,)), ((), ()))
    tn = (((0,), (0,)), ((), ()))

    def visit(i):
        def tile(d):
            return pl.ds(pl.multiple_of((i + SPAN - d) * BLOCK, BLOCK), BLOCK)

        mine_rows = pl.ds(pl.multiple_of(i * BLOCK, BLOCK), BLOCK)
        off = [meta_s[i, 0, 2 * BLOCK + a] for a in range(2)]
        q = jnp.concatenate([q_ref[mine_rows, :HEAD], q_ref[mine_rows, HEAD:]], axis=0)
        up = jnp.concatenate([up_ref[mine_rows, :HEAD], up_ref[mine_rows, HEAD:]], axis=0)

        def listed(which):
            picked = [jnp.zeros((BLOCK, HEAD), jnp.bfloat16) for _ in range(2)]
            for d in range(1, SPAN + 1):
                here = kv[which, tile(d), :]
                picked = [jnp.where(off[a] == d, here, picked[a]) for a in range(2)]
            return jnp.concatenate([kv[which, tile(0), :]] + picked, axis=0)

        k, v = listed(0), listed(1)
        scores = lax.dot_general(k, q, nt, preferred_element_type=jnp.float32)
        sens = lax.dot_general(v, up, nt, preferred_element_type=jnp.float32)
        lo_row = meta[i, :, 0:BLOCK].astype(jnp.float32)
        hi_row = meta[i, :, BLOCK:2 * BLOCK].astype(jnp.float32)
        hi_col = jnp.broadcast_to(hi_row, (BLOCK, BLOCK)).T
        seen = (key_at <= query_at) & (lo_row <= hi_col)
        seen = jnp.concatenate([seen, seen], axis=1)
        low = -jnp.inf
        scores = jnp.concatenate(
            [jnp.where(seen, scores[:BLOCK], low)]
            + [scores[BLOCK * (1 + a):BLOCK * (2 + a)] + jnp.where(off[a] > 0, 0.0, low) for a in range(2)], axis=0)
        top = jnp.max(scores, axis=0, keepdims=True)
        exps = jnp.exp2((scores - top) * scale)
        inverse = 1.0 / jnp.sum(exps, axis=0, keepdims=True)
        probs = exps * inverse
        delta = jnp.sum(probs * sens, axis=0, keepdims=True)
        weights = probs.astype(jnp.bfloat16)
        slopes = (probs * (sens - delta)).astype(jnp.bfloat16)
        dq = lax.dot_general(slopes, k, tn, preferred_element_type=jnp.float32) * factor
        dq_ref[mine_rows, :HEAD] = dq[:BLOCK].astype(jnp.bfloat16)
        dq_ref[mine_rows, HEAD:] = dq[BLOCK:].astype(jnp.bfloat16)
        for which, (left_side, right_side) in enumerate(((slopes, q), (weights, up))):
            grad = jnp.dot(left_side, right_side, preferred_element_type=jnp.float32)
            acc[which, tile(0), :] += grad[:BLOCK]
            for d in range(1, SPAN + 1):
                term = jnp.where(off[1] == d, grad[2 * BLOCK:], 0.0)
                term = jnp.where(off[0] == d, grad[BLOCK:2 * BLOCK], term)
                acc[which, tile(d), :] += term

    def total(slot, c):
        return (part_buf[slot, part(c)].astype(jnp.float32)
                + chain_buf[slot, part(c)].astype(jnp.float32)).astype(jnp.bfloat16)

    def bown_start(g):
        j = back_at(g)

        @when(zh % 2 == 1)
        def _():
            back_left(j).start()

        @when(zh % 2 == 0)
        def _():
            back_right(j).start()

    def bown_sent(g):
        j = back_at(g)

        @when(zh % 2 == 1)
        def _():
            back_left(j).wait_send()

        @when(zh % 2 == 0)
        def _():
            back_right(j).wait_send()

    first_compute = nhalo + LANDED
    last_compute = first_compute + n - 1
    first_give = first_compute + nhalo
    first_back = first_give + 2
    backs = (last_compute - first_back) // 2 + 1
    steps = last_compute + 1 + n + BACK_END - backs

    def step(t, carry):
        @when((t >= WINDOW) & (t < n + WINDOW))
        def _():
            own_sent(t - WINDOW)

        @when(t < n)
        def _():
            own_start(t)

        for slot in range(2):
            k = t - jnp.where(zh == 3 - 3 * slot, RELAYED, ARRIVE)

            @when((k >= 0) & (k < n))
            def _():
                c = chunk_at(k)

                @when(zh != 3 * slot)
                def _():
                    wait_for(unit.at[slot, part(c)], chain_recv.at[slot, c])

                @when(zh == 2 - slot)
                def _():
                    (right if slot == 0 else left)(c).start()

                @when(y == HOME[slot])
                def _():
                    stay(slot, c).start()

                @when(y != HOME[slot])
                def _():
                    along_y(slot, c).start()

        u = jnp.where(t > last_compute, backs + t - last_compute - 1, (t - first_back) // 2)
        turn = (t > last_compute) | ((t >= first_back) & ((t - first_back) % 2 == 0))

        @when(t == 2)
        def _():
            for i in range(1, 4):
                wait_for(meta.at[y * 4 + (zh + 4 - i) % 4], meta_z_recv.at[i - 1])
            for i in range(1, 4):
                meta_y(i).start()

        @when(turn & (u >= BACK_WINDOW) & (u < n + BACK_WINDOW))
        def _():
            bown_sent(u - BACK_WINDOW)

        @when(turn & (u < n))
        def _():
            j = back_at(u)
            for slot in range(2):
                wait_for(part_buf.at[slot, part(j)], yb_recv.at[slot, j])
            bown_start(u)

        @when(turn & (u < n))
        def _():
            c = chunk_at(u)

            @when(zh == 2)
            def _():
                right(c).wait_send()

            @when(zh == 1)
            def _():
                left(c).wait_send()

            for slot in range(2):
                @when(y != HOME[slot])
                def _():
                    along_y(slot, c).wait_send()

            @when(u < nhalo)
            def _():
                to_next(nhalo - 1 - u).wait_send()

        @when((t >= LANDED) & (t < n + LANDED))
        def _():
            k = t - LANDED
            c = chunk_at(k)
            for which in range(2):
                wait_for(landing(which, c), kv_recv.at[which, c])

            @when(k < nhalo)
            def _():
                to_next(nhalo - 1 - k).start()

        @when(t == first_compute)
        def _():
            for i in range(1, 4):
                wait_for(meta.at[pl.ds(4 * ((y + 4 - i) % 4), 4)], meta_y_recv.at[i - 1])
            copy = pltpu.make_async_copy(meta, meta_s, load_sem.at[3])
            copy.start()
            load_q.wait()
            load_up.wait()
            copy.wait()

        @when((t >= first_compute) & (t <= last_compute))
        def _():
            i = last_compute - t

            @when(i < nhalo)
            def _():
                wait_for(kv.at[:, part(i)], halo_recv.at[i])

            for b in range(CHUNK // BLOCK):
                visit(i * (CHUNK // BLOCK) + b)

        @when(t == last_compute)
        def _():
            for piece in range(nhalo)[::-1]:
                for which in range(2):
                    scaled = acc[which, part(piece)] * (factor if which == 0 else 1.0)
                    halo_out[which, part(piece)] = scaled.astype(jnp.bfloat16)
                to_before(piece).start()

        @when(turn & (u >= BACK_RELAY) & (u < n + BACK_RELAY))
        def _():
            j = back_at(u - BACK_RELAY)

            @when(zh == 2)
            def _():
                wait_for(chain_buf.at[0, part(j)], bchain_recv.at[0, j])
                part_buf[0, part(j)] = total(0, j)
                back_left(j).start()

            @when(zh == 1)
            def _():
                wait_for(chain_buf.at[1, part(j)], bchain_recv.at[1, j])
                part_buf[1, part(j)] = total(1, j)
                back_right(j).start()

        gives_early = (t >= first_give) & (t < first_give + n - nhalo)
        gives_late = turn & (u + 2 >= n - nhalo) & (u + 2 < n)

        @when(gives_early | gives_late)
        def _():
            j = back_at(jnp.where(gives_late, u + 2, t - first_give))

            @when(j >= n - nhalo)
            def _():
                piece = j - (n - nhalo)
                wait_for(halo_in.at[:, part(piece)], hback_recv.at[piece])

            for which in range(2):
                scaled = acc[which, part(j + nhalo)] * (factor if which == 0 else 1.0)

                @when(j < n - nhalo)
                def _():
                    back[which, part(j)] = scaled.astype(jnp.bfloat16)

                @when(j >= n - nhalo)
                def _():
                    piece = j - (n - nhalo)
                    back[which, part(j)] = (
                        scaled + halo_in[which, part(piece)].astype(jnp.float32)).astype(jnp.bfloat16)

                @when(y == HOME[which])
                def _():
                    back_stay(which, j).start()

                @when(y != HOME[which])
                def _():
                    back_y(which, j).start()

        @when(turn & (u >= BACK_END))
        def _():
            j = back_at(u - BACK_END)
            for which in range(2):
                @when(y != HOME[which])
                def _():
                    back_y(which, j).wait_send()

            @when(u - BACK_END >= n - nhalo)
            def _():
                to_before(u - BACK_END - (n - nhalo)).wait_send()

            @when(zh <= 1)
            def _():
                wait_for(chain_buf.at[0, part(j)], bchain_recv.at[0, j])

            @when(zh >= 2)
            def _():
                wait_for(chain_buf.at[1, part(j)], bchain_recv.at[1, j])

            @when(zh == 0)
            def _():
                dkv_ref[part(j)] = total(0, j)

            @when(zh == 1)
            def _():
                dkv_ref[part(j)] = chain_buf[0, part(j)]

            @when(zh == 2)
            def _():
                dkv_ref[part(j)] = chain_buf[1, part(j)]

            @when(zh == 3)
            def _():
                dkv_ref[part(j)] = total(1, j)

        return carry

    lax.fori_loop(0, steps, step, 0)

    for i in range(1, 4):
        meta_z(i).wait_send()
        meta_y(i).wait_send()

    def drain(k, carry):
        @when(zh == 2)
        def _():
            back_left(k).wait_send()

        @when(zh == 1)
        def _():
            back_right(k).wait_send()

        return carry

    lax.fori_loop(0, n, drain, 0)


def solution(mesh):
    ns, nh = mesh.shape["seq"], mesh.shape["head"]

    def on_device(queries, key_value_rows, upstream, ancestors, valid, span_lo, span_hi):
        rows = queries.shape[0]
        halo = SPAN * BLOCK
        n, nhalo = rows // CHUNK, halo // CHUNK
        hbm = pl.BlockSpec(memory_space=pl.ANY)
        vmem = pl.BlockSpec(memory_space=pltpu.VMEM)
        smem = pl.BlockSpec(memory_space=pltpu.SMEM)
        dma = pltpu.SemaphoreType.DMA
        bf16, f32 = jnp.bfloat16, jnp.float32
        return pl.pallas_call(
            functools.partial(kernel, ns, nh, rows),
            out_shape=(jax.ShapeDtypeStruct(queries.shape, bf16), jax.ShapeDtypeStruct((rows, HEAD), bf16)),
            in_specs=[hbm, hbm, hbm, vmem, vmem, smem, smem],
            out_specs=(vmem, vmem),
            scratch_shapes=[
                pltpu.VMEM((3, rows, HEAD), bf16), pltpu.VMEM((2, halo + rows, HEAD), bf16),
                pltpu.VMEM((nh, 1, 3 * BLOCK), jnp.int32), pltpu.SMEM((nh, 1, 3 * BLOCK), jnp.int32),
                pltpu.VMEM(queries.shape, bf16), pltpu.VMEM(queries.shape, bf16),
                pltpu.VMEM((2, halo + rows, HEAD), f32), pltpu.VMEM((2, rows, HEAD), bf16),
                pltpu.VMEM((2, halo, HEAD), bf16), pltpu.VMEM((2, halo, HEAD), bf16),
                pltpu.VMEM((2, rows, HEAD), bf16), pltpu.VMEM((2, rows, HEAD), bf16),
                dma((4,)), dma((3,)), dma((3,)), dma((3,)), dma((3,)),
                dma((n,)), dma((n,)), dma((2, n)), dma((2, n)), dma((2, n)), dma((nhalo,)), dma((nhalo,)),
                dma((nhalo,)), dma((nhalo,)), dma((2, n)), dma((2, n)), dma((n,)), dma((n,)), dma((2, n)),
            ],
            compiler_params=pltpu.CompilerParams(
                collective_id=0, has_side_effects=True, vmem_limit_bytes=VMEM_LIMIT),
            name="tree_attention",
        )(key_value_rows, queries, upstream, span_lo.reshape(1, BLOCK), span_hi.reshape(1, BLOCK), ancestors, valid)

    placed = (P("seq", "head"), P("seq", "head"), P("seq", "head"), P(("seq", "head"), None),
              P(("seq", "head"), None), P(("seq", "head")), P(("seq", "head")))
    return jax.shard_map(on_device, mesh=mesh, in_specs=placed, out_specs=(P("seq", "head"), P("seq", "head")),
                         check_vma=False)
```
